768 devices in a mesh: lon: 192 (over x, z, y_hi, core), tm: 4 (over y_lo).
Axes of the slice: x: 4, y: 8 (y_hi: 2, y_lo: 4; y = y_hi * 4 + y_lo), z: 12, core: 2. Of those that a mesh axis runs over, the one named last changes fastest.
Arguments:
- right_side: float32 [1536, 96, 256], P('lon', 'tm'), may hold values from -40 to 40
- kappa_squared: float32 [1536, 96, 256], P('lon', 'tm'), may hold values from 0.05 to 0.5
- hdiff: float32 [1536, 96, 256], P('lon', 'tm'), may hold values from 0.1 to 0.4
- obs_weight: float32 [1536, 96, 256], P('lon', 'tm'), may hold values from 0.2 to 2
Outputs:
- solution_field: float32 [1536, 96, 256], P('lon', 'tm')
- residual: float32 [1536, 96, 256], P('lon', 'tm')
The draws below stay inside these ranges and needn't reach their ends.
All inputs are finite; a program needn't handle non-finite values.
Results may differ from the reference program's by a relative error of at most 0.033.
Values sent between devices are 32-bit elements; how exact they have to be, the bound alone decides.
A program may use at most 32 MiB of HBM per device.

```python
import math
import jax
import jax.numpy as jnp

NLAT = 256
ITERS = 3
NLON = 1536
NTIME = 96


def draw_right_side(key, part):
    key = jax.random.fold_in(key, 7)
    key_base, key_lat, key_time = jax.random.split(key, 3)
    lon_pos = jnp.arange(NLON, dtype=jnp.float32) / NLON
    rise = jnp.exp(jnp.log(3.0) * lon_pos)[:, None, None]
    lat_scale = jnp.exp(jnp.log(10.0) * jax.random.uniform(key_lat, (NLAT,), jnp.float32))[None, None, :]
    time_scale = jnp.exp(jnp.log(2.0) * jax.random.uniform(key_time, (NTIME,), jnp.float32))[None, :, None]
    base = jax.random.truncated_normal(key_base, -4.0, 4.0, (NLON, NTIME, NLAT), jnp.float32)
    values = base * rise * lat_scale * time_scale / 6.0
    return values.astype(jnp.float32)


def shard_levels(stream_key, dims, cuts, smallest, high):
    gain = 1.0
    for axis_at, parts in cuts:
        heights = jax.random.uniform(jax.random.fold_in(jax.random.fold_in(stream_key, 6), axis_at), (parts,), jnp.float32, smallest / len(cuts), high / len(cuts))
        gain = gain * jnp.repeat(jnp.exp(heights), dims[axis_at] // parts).reshape((-1,) + (1,) * (len(dims) - 1 - axis_at))
    return gain


def setup_inputs(seed: int = 0) -> dict:
    keys = jax.random.split(jax.random.key(seed), 5)
    return {
        "right_side": draw_right_side(jax.random.fold_in(keys[4], 71), 0),
        "kappa_squared": jnp.clip(jnp.exp(math.log(0.5) - 2.3025851 * jax.random.uniform(keys[1], (NLON, NTIME, NLAT), jnp.float32) ** shard_levels(keys[1], (NLON, NTIME, NLAT), ((0, 192), (1, 4)), -0.2, 0.2)), 0.05, 0.5),
        "hdiff": jnp.clip(jnp.exp(math.log(0.4) - 1.3862944 * jax.random.uniform(keys[2], (NLON, NTIME, NLAT), jnp.float32) ** shard_levels(keys[2], (NLON, NTIME, NLAT), ((0, 192), (1, 4)), -0.2, 0.2)), 0.1, 0.4),
        "obs_weight": jnp.clip(jnp.exp(math.log(2.0) - 2.3025851 * jax.random.uniform(keys[3], (NLON, NTIME, NLAT), jnp.float32) ** shard_levels(keys[3], (NLON, NTIME, NLAT), ((0, 192), (1, 4)), -0.2, 0.2)), 0.2, 2.0),
    }


def face(here, there):
    total = here + there
    safe = jnp.where(total > 0, total, 1.0)
    return jnp.where(total > 0, 2.0 * here * there / safe, 0.0)


def lat_next(a, step):
    zeros = jnp.zeros_like(a[:, :, :1])
    if step > 0:
        return jnp.concatenate([a[:, :, 1:], zeros], axis=2)
    return jnp.concatenate([zeros, a[:, :, :-1]], axis=2)


def face_set(hpad):
    middle_part = hpad[1:-1, 1:-1]
    return (face(middle_part, hpad[2:, 1:-1]), face(middle_part, hpad[:-2, 1:-1]),
            face(middle_part, hpad[1:-1, 2:]), face(middle_part, hpad[1:-1, :-2]),
            face(middle_part, lat_next(middle_part, 1)), face(middle_part, lat_next(middle_part, -1)))


def stencil_apply(vector_padded, kappa_field, face_values):
    middle_part = vector_padded[1:-1, 1:-1]
    remaining_terms = (vector_padded[2:, 1:-1], vector_padded[:-2, 1:-1], vector_padded[1:-1, 2:], vector_padded[1:-1, :-2],
              lat_next(middle_part, 1), lat_next(middle_part, -1))
    total = kappa_field * middle_part
    for coeff, other in zip(face_values, remaining_terms):
        total = total + coeff * (middle_part - other)
    return total


def pad_grid(a):
    a = jnp.pad(a, ((1, 1), (0, 0), (0, 0)), mode="wrap")
    return jnp.pad(a, ((0, 0), (1, 1), (0, 0)))


def reference(right_side, kappa_squared, hdiff, obs_weight):
    face_values = face_set(pad_grid(hdiff))
    diag_l = kappa_squared + face_values[0] + face_values[1] + face_values[2] + face_values[3] + face_values[4] + face_values[5]
    squares = face_values[0] ** 2 + face_values[1] ** 2 + face_values[2] ** 2 + face_values[3] ** 2 + face_values[4] ** 2 + face_values[5] ** 2
    inverse = 1.0 / (diag_l * diag_l + squares + obs_weight)

    def precision(vector_input):
        once = stencil_apply(pad_grid(vector_input), kappa_squared, face_values)
        return stencil_apply(pad_grid(once), kappa_squared, face_values) + obs_weight * vector_input

    solution_field = jnp.zeros_like(right_side)
    residual = right_side
    scaled = inverse * residual
    direction = scaled
    rz_now = jnp.sum(residual * scaled)
    for step in range(ITERS):
        image = precision(direction)
        alpha = rz_now / jnp.sum(direction * image)
        solution_field = solution_field + alpha * direction
        residual = residual - alpha * image
        scaled = inverse * residual
        rz_next = jnp.sum(residual * scaled)
        direction = scaled + (rz_next / rz_now) * direction
        rz_now = rz_next
    return solution_field, residual
```

```python
import itertools

import jax
import jax.numpy as jnp
from jax import lax
from jax.experimental import pallas as pl
from jax.experimental.pallas import tpu as pltpu
from jax.sharding import PartitionSpec as P

MESH = pl.DeviceIdType.MESH
SIZES = {"x": 4, "z": 12, "h": 2, "c": 2, "l": 4}
STAGES = (("z", "c"), ("x", "h", "l"))
NX, NT, NA = 8, 24, 256
HX, HT = 3, 8
EX, ET = NX + 2 * HX, NT + 2 * HT
T0, T1 = HT, HT + NT


def place():
    lon, tm = lax.axis_index("lon"), lax.axis_index("tm")
    return {"c": lon % 2, "h": (lon // 2) % 2, "z": (lon // 4) % 12, "x": lon // 48, "l": tm}


def peers(axes):
    here, out = place(), []
    for offset in itertools.product(*[range(SIZES[a]) for a in axes]):
        if any(offset):
            at = dict(here)
            for a, o in zip(axes, offset):
                if o:
                    at[a] = lax.rem(at[a] + o, SIZES[a])
            out.append((((at["x"] * 12 + at["z"]) * 2 + at["h"]) * 2 + at["c"], at["l"]))
    return out


def face(here, there):
    total = here + there
    return jnp.where(total > 0, 2.0 * here * there / jnp.where(total > 0, total, 1.0), 0.0)


def roll(v, step, axis):
    return pltpu.roll(v, step % v.shape[axis], axis)


def solve_kernel(b_in, k_in, h_in, o_in, x_out, r_out, b, k, h, o, fx, ft, fl, d, m,
                 y0, y1, y2, u, v, w1, w2, w3, row, slots,
                 in_sem, s1, r1, s2, r2, s3, r3, sa, ra):
    lon, tm = lax.axis_index("lon"), lax.axis_index("tm")
    east, west = lax.rem(lon + 1, 192), lax.rem(lon + 191, 192)
    up, down = lax.rem(tm + 1, 4), lax.rem(tm + 3, 4)
    stage_peers = [peers(axes) for axes in STAGES]

    barrier = pltpu.get_barrier_semaphore()
    everyone = [(a, t) for a in (east, west) for t in (tm, up, down)] + [(lon, up), (lon, down)]
    for group in stage_peers:
        everyone += group
    for who in everyone:
        pl.semaphore_signal(barrier, inc=1, device_id=who, device_id_type=MESH)

    mine = [
        pltpu.make_async_copy(src, dst.at[pl.ds(HX, NX), pl.ds(T0, NT)], in_sem.at[i])
        for i, (src, dst) in enumerate(((b_in, b), (k_in, k), (h_in, h), (o_in, o)))
    ]
    for copy in mine:
        copy.start()

    @pl.when(tm == 0)
    def _():
        for ref, value in ((h, 0.0), (k, 1.0), (o, 1.0), (b, 0.0), (y1, 0.0), (v, 0.0)):
            ref[:, :T0] = jnp.full((EX, HT, NA), value, jnp.float32)

    @pl.when(tm == 3)
    def _():
        for ref, value in ((h, 0.0), (k, 1.0), (o, 1.0), (b, 0.0), (y1, 0.0), (v, 0.0)):
            ref[:, T1:] = jnp.full((EX, HT, NA), value, jnp.float32)

    pl.semaphore_wait(barrier, len(everyone))

    def exchange(src, off_x, off_t, dst, width, corner, ssem, rsem, base):
        plain, upward, downward = [], [], []
        count = itertools.count(base)

        def make(group, sx, st, nx, nt, dx, dt, who):
            n = next(count)
            group.append(pltpu.make_async_remote_copy(
                src.at[pl.ds(off_x + sx, nx), pl.ds(off_t + st, nt)],
                dst.at[pl.ds(dx, nx), pl.ds(dt, nt)],
                ssem.at[n], rsem.at[n], device_id=who, device_id_type=MESH))

        make(plain, NX - width, 0, width, NT, HX - width, T0, (east, tm))
        make(plain, 0, 0, width, NT, HX + NX, T0, (west, tm))
        make(upward, 0, NT - width, NX, width, HX, T0 - width, (lon, up))
        make(downward, 0, 0, NX, width, HX, T1, (lon, down))
        if corner:
            make(upward, NX - corner, NT - corner, corner, corner, HX - corner, T0 - corner, (east, up))
            make(upward, 0, NT - corner, corner, corner, HX + NX, T0 - corner, (west, up))
            make(downward, NX - corner, 0, corner, corner, HX - corner, T1, (east, down))
            make(downward, 0, 0, corner, corner, HX + NX, T1, (west, down))
        return plain, upward, downward, next(count)

    def start(groups):
        plain, upward, downward = groups[:3]
        for copy in plain:
            copy.start()

        @pl.when(tm < 3)
        def _():
            for copy in upward:
                copy.start()

        @pl.when(tm > 0)
        def _():
            for copy in downward:
                copy.start()

    def received(groups):
        plain, upward, downward = groups[:3]
        for copy in plain:
            copy.wait_recv()

        @pl.when(tm > 0)
        def _():
            for copy in upward:
                copy.wait_recv()

        @pl.when(tm < 3)
        def _():
            for copy in downward:
                copy.wait_recv()

    def sent(groups):
        plain, upward, downward = groups[:3]
        for copy in plain:
            copy.wait_send()

        @pl.when(tm < 3)
        def _():
            for copy in upward:
                copy.wait_send()

        @pl.when(tm > 0)
        def _():
            for copy in downward:
                copy.wait_send()

    first, base = [], 0
    for src, dst, width, corner in ((h_in, h, 3, 2), (k_in, k, 2, 1), (o_in, o, 2, 1), (b_in, b, 2, 1)):
        groups = exchange(src, 0, 0, dst, width, corner, s1, r1, base)
        base = groups[3]
        first.append(groups)
    for groups in first:
        start(groups)
    for copy in mine:
        copy.wait()
    for groups in first:
        received(groups)

    def stencil(field, s):
        here = field[s]
        ftv, flv = ft[s], fl[s]
        near = fx[s] * field[s + 1] + fx[s - 1] * field[s - 1]
        near += ftv * roll(here, -1, 0) + roll(ftv * here, 1, 0)
        near += flv * roll(here, -1, 1) + roll(flv * here, 1, 1)
        return d[s] * here - near

    lat = lax.broadcasted_iota(jnp.int32, (ET, NA), 1)

    @pl.loop(0, EX - 1)
    def _(s):
        fx[s] = face(h[s], h[s + 1])

    @pl.loop(1, EX - 1)
    def _(s):
        here = h[s]
        ftv = face(here, roll(here, -1, 0))
        flv = jnp.where(lat == NA - 1, 0.0, face(here, roll(here, -1, 1)))
        ft[s], fl[s] = ftv, flv
        sides = (fx[s], fx[s - 1], ftv, roll(ftv, 1, 0), flv, roll(flv, 1, 1))
        total, squares = k[s], o[s]
        for f in sides:
            total += f
            squares += f * f
        d[s] = total
        inverse = 1.0 / (total * total + squares)
        m[s] = inverse
        y0[s] = inverse * b[s]

    @pl.loop(2, EX - 2)
    def _(s):
        u[s] = stencil(y0, s)

    @pl.loop(HX, HX + NX)
    def _(s):
        w = (stencil(u, s) + o[s] * y0[s])[T0:T1]
        w1[s - HX] = w
        y1[s, T0:T1] = m[s, T0:T1] * w

    second = exchange(y1, HX, T0, y1, 3, 2, s2, r2, 0)
    start(second)
    received(second)

    @pl.loop(1, EX - 1)
    def _(s):
        u[s] = stencil(y1, s)

    @pl.loop(2, EX - 2)
    def _(s):
        w = stencil(u, s) + o[s] * y1[s]
        w2[s] = w
        y2[s] = m[s] * w

    zero = jnp.zeros((NT, NA), jnp.float32)

    def moments(s, sums):
        w = stencil(y2, s)[T0:T1]
        v[s, T0:T1] = w
        bb, yy0, yy1, yy2 = b[s, T0:T1], y0[s, T0:T1], y1[s, T0:T1], y2[s, T0:T1]
        ww1, ww2 = w1[s - HX], w2[s, T0:T1]
        terms = (bb * yy0, yy0 * ww1, ww1 * yy1, ww1 * yy2, ww2 * yy2, w * w + o[s, T0:T1] * yy2 * yy2)
        return tuple(a + t for a, t in zip(sums, terms))

    sums = lax.fori_loop(HX, HX + NX, moments, (zero,) * 6)

    third = exchange(v, HX, T0, v, 1, 0, s3, r3, 0)
    start(third)

    lane = lax.broadcasted_iota(jnp.int32, (1, 128), 1)
    packed = jnp.zeros((1, 128), jnp.float32)
    for i, part in enumerate(sums):
        packed = jnp.where(lane == i, jnp.sum(part, keepdims=True), packed)

    all_copies = []
    for stage, group in enumerate(stage_peers):
        row[pl.ds(stage, 1)] = packed
        copies = [
            pltpu.make_async_remote_copy(
                row.at[pl.ds(stage, 1)], slots.at[stage, pl.ds(i, 1)], sa.at[stage, i], ra.at[stage, i],
                device_id=who, device_id_type=MESH)
            for i, who in enumerate(group)
        ]
        for copy in copies:
            copy.start()
        all_copies += copies
        if stage == 0:
            received(third)

            @pl.loop(HX, HX + NX)
            def _(s):
                w3[s - HX] = (stencil(v, s) + o[s] * y2[s])[T0:T1]

        for copy in copies:
            copy.wait_recv()
        packed = packed + jnp.sum(slots[stage, : len(group)], axis=0, keepdims=True)

    mu = [packed[:, i : i + 1] for i in range(6)]

    def form(c, shift):
        total = 0.0
        for i, a in enumerate(c):
            for j, e in enumerate(c):
                total = total + a * e * mu[i + j + shift]
        return total

    a0 = mu[0] / mu[1]
    rho1 = [jnp.ones_like(a0), -a0]
    rz1 = form(rho1, 0)
    beta0 = rz1 / mu[0]
    p1 = [1.0 + beta0, -a0]
    a1 = rz1 / form(p1, 1)
    rho2 = [jnp.ones_like(a0), -a0 - a1 * p1[0], -a1 * p1[1]]
    rz2 = form(rho2, 0)
    beta1 = rz2 / rz1
    p2 = [rho2[0] + beta1 * p1[0], rho2[1] + beta1 * p1[1], rho2[2]]
    a2 = rz2 / form(p2, 1)
    c0 = a0 + a1 * p1[0] + a2 * p2[0]
    c1 = a1 * p1[1] + a2 * p2[1]
    c2 = a2 * p2[2]

    @pl.loop(0, NX)
    def _(s):
        e = s + HX
        x_out[s] = c0 * y0[e, T0:T1] + c1 * y1[e, T0:T1] + c2 * y2[e, T0:T1]
        r_out[s] = b[e, T0:T1] - (c0 * w1[s] + c1 * w2[e, T0:T1] + c2 * w3[s])

    for groups in first:
        sent(groups)
    sent(second)
    sent(third)
    for copy in all_copies:
        copy.wait_send()


def body(right_side, kappa_squared, hdiff, obs_weight):
    wide = pltpu.VMEM((EX, ET, NA), jnp.float32)
    block = pltpu.VMEM((NX, NT, NA), jnp.float32)
    most = max(len(list(itertools.product(*[range(SIZES[a]) for a in axes]))) for axes in STAGES)
    dma = pltpu.SemaphoreType.DMA
    return pl.pallas_call(
        solve_kernel,
        out_shape=(jax.ShapeDtypeStruct((NX, NT, NA), jnp.float32),) * 2,
        in_specs=[pl.BlockSpec(memory_space=pl.ANY)] * 4,
        out_specs=(pl.BlockSpec(memory_space=pltpu.VMEM),) * 2,
        scratch_shapes=[wide] * 14 + [block] + [wide] + [block]
        + [pltpu.VMEM((8, 128), jnp.float32), pltpu.VMEM((len(STAGES), most, 128), jnp.float32)]
        + [dma((4,)), dma((32,)), dma((32,)), dma((8,)), dma((8,)), dma((4,)), dma((4,)),
           dma((len(STAGES), most)), dma((len(STAGES), most))],
        compiler_params=pltpu.CompilerParams(
            collective_id=0, has_side_effects=True, vmem_limit_bytes=40 * 2**20
        ),
    )(right_side, kappa_squared, hdiff, obs_weight)


def solution(mesh):
    placed = P("lon", "tm", None)
    return jax.shard_map(
        body, mesh=mesh, in_specs=(placed,) * 4, out_specs=(placed,) * 2, check_vma=False
    )
```

```python
import itertools

import jax
import jax.numpy as jnp
from jax import lax
from jax.experimental import pallas as pl
from jax.experimental.pallas import tpu as pltpu
from jax.sharding import PartitionSpec as P

MESH = pl.DeviceIdType.MESH
SIZES = {"x": 4, "z": 12, "h": 2, "c": 2, "l": 4}
STAGES = (("z", "c"), ("x", "h", "l"))
NX, NT, NA = 8, 24, 256
HX, HT = 3, 8
EX, ET = NX + 2 * HX, NT + 2 * HT
T0, T1 = HT, HT + NT


def place():
    lon, tm = lax.axis_index("lon"), lax.axis_index("tm")
    return {"c": lon % 2, "h": (lon // 2) % 2, "z": (lon // 4) % 12, "x": lon // 48, "l": tm}


def peers(axes):
    here, out = place(), []
    for offset in itertools.product(*[range(SIZES[a]) for a in axes]):
        if any(offset):
            at = dict(here)
            for a, o in zip(axes, offset):
                if o:
                    at[a] = lax.rem(at[a] + o, SIZES[a])
            out.append((((at["x"] * 12 + at["z"]) * 2 + at["h"]) * 2 + at["c"], at["l"]))
    return out


def face(here, there):
    total = here + there
    return jnp.where(total > 0, 2.0 * here * there / jnp.where(total > 0, total, 1.0), 0.0)


def roll(v, step, axis):
    return pltpu.roll(v, step % v.shape[axis], axis)


def solve_kernel(b_in, k_in, h_in, o_in, x_out, r_out,
                 b, k, h, o, fx, ft, fl, d, m, y0, y1, y2, u, v, w1, w2, w3, row, slots,
                 in_sem, s_tm, r_tm, s_lon, r_lon, s_cor, r_cor, sa, ra):
    lon, tm = lax.axis_index("lon"), lax.axis_index("tm")
    east, west = lax.rem(lon + 1, 192), lax.rem(lon + 191, 192)
    up, down = lax.rem(tm + 1, 4), lax.rem(tm + 3, 4)

    barrier = pltpu.get_barrier_semaphore()
    near = [(east, tm), (west, tm), (lon, up), (lon, down), (east, up), (east, down), (west, up), (west, down)]
    for who in near:
        pl.semaphore_signal(barrier, inc=1, device_id=who, device_id_type=MESH)

    mine = [
        pltpu.make_async_copy(src, dst.at[pl.ds(HX, NX), pl.ds(T0, NT)], in_sem.at[i])
        for i, (src, dst) in enumerate(((b_in, b), (k_in, k), (h_in, h), (o_in, o)))
    ]
    for copy in mine:
        copy.start()

    stage_peers = [peers(axes) for axes in STAGES]
    for group in stage_peers:
        for who in group:
            pl.semaphore_signal(barrier, inc=1, device_id=who, device_id_type=MESH)

    edges = ((h, 0.0), (k, 1.0), (o, 1.0), (b, 0.0), (y1, 0.0), (v, 0.0))

    @pl.when(tm == 0)
    def _():
        for ref, value in edges:
            ref[:, :T0] = jnp.full((EX, HT, NA), value, jnp.float32)

    @pl.when(tm == 3)
    def _():
        for ref, value in edges:
            ref[:, T1:] = jnp.full((EX, HT, NA), value, jnp.float32)

    pl.semaphore_wait(barrier, len(near) + sum(map(len, stage_peers)))

    def remote(src, dst, ssem, rsem, who):
        return pltpu.make_async_remote_copy(src, dst, ssem, rsem, device_id=who, device_id_type=MESH)

    class Lon:
        def __init__(self, n, src, off_x, off_t, dst, depth, width=1):
            def part(at):
                return src.at[pl.ds(off_x + at, width), pl.ds(off_t, NT)]

            def halo(at):
                return dst.at[pl.ds(at, width), pl.ds(T0, NT)]

            self.copies = [
                remote(part(NX - depth - width + 1), halo(HX - depth - width + 1),
                       s_lon.at[n, 0], r_lon.at[n, 0], (east, tm)),
                remote(part(depth - 1), halo(HX + NX + depth - 1),
                       s_lon.at[n, 1], r_lon.at[n, 1], (west, tm)),
            ]

        def start(self):
            for copy in self.copies:
                copy.start()

        def received(self):
            for copy in self.copies:
                copy.wait_recv()

        def sent(self):
            for copy in self.copies:
                copy.wait_send()

    class Tm:
        def __init__(self, upward, downward):
            self.upward, self.downward = upward, downward

        def run(self, what, towards, back):
            @pl.when(towards)
            def _():
                for copy in self.upward:
                    getattr(copy, what)()

            @pl.when(back)
            def _():
                for copy in self.downward:
                    getattr(copy, what)()

        def start(self):
            self.run("start", tm < 3, tm > 0)

        def received(self):
            self.run("wait_recv", tm > 0, tm < 3)

        def sent(self):
            self.run("wait_send", tm < 3, tm > 0)

    def rows(n, src, off_x, off_t, dst, width):
        return Tm(
            [remote(src.at[pl.ds(off_x, NX), pl.ds(off_t + NT - width, width)],
                    dst.at[pl.ds(HX, NX), pl.ds(T0 - width, width)], s_tm.at[n, 0], r_tm.at[n, 0], (lon, up))],
            [remote(src.at[pl.ds(off_x, NX), pl.ds(off_t, width)],
                    dst.at[pl.ds(HX, NX), pl.ds(T1, width)], s_tm.at[n, 1], r_tm.at[n, 1], (lon, down))],
        )

    def corners(n, src, off_x, off_t, dst, width):
        def make(i, sx, st, dx, dt, who):
            return remote(src.at[pl.ds(off_x + sx, width), pl.ds(off_t + st, width)],
                          dst.at[pl.ds(dx, width), pl.ds(dt, width)], s_cor.at[n, i], r_cor.at[n, i], who)

        return Tm(
            [make(0, NX - width, NT - width, HX - width, T0 - width, (east, up)),
             make(1, 0, NT - width, HX + NX, T0 - width, (west, up))],
            [make(2, NX - width, 0, HX - width, T1, (east, down)),
             make(3, 0, 0, HX + NX, T1, (west, down))],
        )

    inputs = ((h_in, h), (k_in, k), (o_in, o), (b_in, b))
    tm_first = [rows(i, src, 0, 0, dst, 3 if i == 0 else 2) for i, (src, dst) in enumerate(inputs)]
    lon_first = [Lon(i, src, 0, 0, dst, 1, 2 if i == 0 else 1) for i, (src, dst) in enumerate(inputs)]
    cor_first = [corners(i, src, 0, 0, dst, 2 if i == 0 else 1) for i, (src, dst) in enumerate(inputs)]
    lon_y0 = Lon(4, y0, HX, T0, y0, 2)
    lon_late = [Lon(5, h_in, 0, 0, h, 3), Lon(6, k_in, 0, 0, k, 2)]

    tm_first[0].start()
    lon_first[0].start()
    for i in (1, 2, 3):
        tm_first[i].start()
    for i in (1, 2, 3):
        lon_first[i].start()
    for copies in cor_first:
        copies.start()

    lat = lax.broadcasted_iota(jnp.int32, (ET, NA), 1)

    def stencil(field, s):
        here = field[s]
        ftv, flv = ft[s], fl[s]
        sides = fx[s] * field[s + 1] + fx[s - 1] * field[s - 1]
        sides += ftv * roll(here, -1, 0) + roll(ftv * here, 1, 0)
        sides += flv * roll(here, -1, 1) + roll(flv * here, 1, 1)
        return d[s] * here - sides

    def across(*slabs):
        for s in slabs:
            fx[s] = face(h[s], h[s + 1])

    def within(*slabs):
        for s in slabs:
            here = h[s]
            ft[s] = face(here, roll(here, -1, 0))
            fl[s] = jnp.where(lat == NA - 1, 0.0, face(here, roll(here, -1, 1)))

    def diagonal(*slabs, full=True):
        for s in slabs:
            ftv, flv = ft[s], fl[s]
            around = (fx[s], fx[s - 1], ftv, roll(ftv, 1, 0), flv, roll(flv, 1, 1))
            total = k[s]
            for f in around:
                total += f
            d[s] = total
            if full:
                squares = o[s]
                for f in around:
                    squares += f * f
                inverse = 1.0 / (total * total + squares)
                m[s] = inverse
                y0[s] = inverse * b[s]

    def apply(src, *slabs):
        for s in slabs:
            u[s] = stencil(src, s)

    def next_first(*slabs):
        for s in slabs:
            w = (stencil(u, s) + o[s] * y0[s])[T0:T1]
            w1[s - HX] = w
            y1[s, T0:T1] = m[s, T0:T1] * w

    def next_second(*slabs):
        for s in slabs:
            w = stencil(u, s) + o[s] * y1[s]
            w2[s] = w
            y2[s] = m[s] * w

    for copy in mine:
        copy.wait()
    for copies in tm_first:
        copies.received()
    across(3, 4, 8, 9)
    within(4, 9)
    diagonal(4, 9)
    lon_y0.start()
    for copies in lon_late:
        copies.start()
    across(5, 6, 7)
    within(3, 5, 6, 7, 8, 10)
    diagonal(5, 6, 7, 8)
    apply(y0, 5, 6, 7, 8)
    next_first(6, 7)

    lon_first[0].received()
    cor_first[0].received()
    across(1, 2, 10, 11)
    within(2, 11)
    diagonal(3, 10)
    apply(y0, 4, 9)
    next_first(5, 8)
    for i in (1, 2, 3):
        lon_first[i].received()
        cor_first[i].received()
    diagonal(2, 11)
    apply(y0, 3, 10)
    next_first(4, 9)
    lon_y0.received()
    apply(y0, 2, 11)
    next_first(3, 10)

    lon_y1 = Lon(7, y1, HX, T0, y1, 1, 3)
    tm_y1 = rows(4, y1, HX, T0, y1, 3)
    cor_y1 = corners(4, y1, HX, T0, y1, 2)
    lon_y1.start()
    tm_y1.start()
    cor_y1.start()

    for copies in lon_late:
        copies.received()
    across(0, 12)
    within(1, 12)
    diagonal(1, 12, full=False)
    tm_y1.received()
    apply(y1, 4, 5, 6, 7, 8, 9)
    next_second(5, 6, 7, 8)

    sums = [jnp.zeros((NT, NA), jnp.float32)] * 6

    def moments(*slabs):
        for s in slabs:
            t = stencil(y2, s)[T0:T1]
            v[s, T0:T1] = t
            yy0, yy1, yy2 = y0[s, T0:T1], y1[s, T0:T1], y2[s, T0:T1]
            ww1, ww2 = w1[s - HX], w2[s, T0:T1]
            terms = (b[s, T0:T1] * yy0, yy0 * ww1, ww1 * yy1, ww1 * yy2, ww2 * yy2,
                     t * t + o[s, T0:T1] * yy2 * yy2)
            for i, term in enumerate(terms):
                sums[i] = sums[i] + term

    moments(6, 7)
    lon_y1.received()
    cor_y1.received()
    apply(y1, 1, 2, 3, 10, 11, 12)
    next_second(2, 3, 4, 9, 10, 11)
    moments(3, 4, 5, 8, 9, 10)

    lane = lax.broadcasted_iota(jnp.int32, (1, 128), 1)
    packed = jnp.zeros((1, 128), jnp.float32)
    for i, part in enumerate(sums):
        packed = jnp.where(lane == i, jnp.sum(part, keepdims=True), packed)

    lon_u2 = Lon(8, v, HX, T0, v, 1)
    tm_u2 = rows(5, v, HX, T0, v, 1)
    all_copies = []
    for stage, group in enumerate(stage_peers):
        row[pl.ds(stage, 1)] = packed
        copies = [
            remote(row.at[pl.ds(stage, 1)], slots.at[stage, pl.ds(i, 1)], sa.at[stage, i], ra.at[stage, i], who)
            for i, who in enumerate(group)
        ]
        for copy in copies:
            copy.start()
        all_copies += copies
        if stage == 0:
            lon_u2.start()
            tm_u2.start()
        if stage == 1:
            tm_u2.received()
            lon_u2.received()
            for s in range(HX, HX + NX):
                w3[s - HX] = (stencil(v, s) + o[s] * y2[s])[T0:T1]
        for copy in copies:
            copy.wait_recv()
        packed = packed + jnp.sum(slots[stage, : len(group)], axis=0, keepdims=True)

    mu = [packed[:, i : i + 1] for i in range(6)]

    def form(c, shift):
        total = 0.0
        for i, a in enumerate(c):
            for j, e in enumerate(c):
                total = total + a * e * mu[i + j + shift]
        return total

    a0 = mu[0] / mu[1]
    rho1 = [jnp.ones_like(a0), -a0]
    rz1 = form(rho1, 0)
    beta0 = rz1 / mu[0]
    p1 = [1.0 + beta0, -a0]
    a1 = rz1 / form(p1, 1)
    rho2 = [jnp.ones_like(a0), -a0 - a1 * p1[0], -a1 * p1[1]]
    rz2 = form(rho2, 0)
    beta1 = rz2 / rz1
    p2 = [rho2[0] + beta1 * p1[0], rho2[1] + beta1 * p1[1], rho2[2]]
    a2 = rz2 / form(p2, 1)
    c = (a0 + a1 * p1[0] + a2 * p2[0], a1 * p1[1] + a2 * p2[1], a2 * p2[2])
    c0, c1, c2 = (jnp.broadcast_to(value, (NT, NA)) for value in c)
    for s in range(NX):
        e = s + HX
        x_out[s] = c0 * y0[e, T0:T1] + c1 * y1[e, T0:T1] + c2 * y2[e, T0:T1]
        r_out[s] = b[e, T0:T1] - (c0 * w1[s] + c1 * w2[e, T0:T1] + c2 * w3[s])

    for copies in tm_first + lon_first + cor_first + lon_late + [lon_y0, lon_y1, tm_y1, cor_y1, lon_u2, tm_u2]:
        copies.sent()
    for copy in all_copies:
        copy.wait_send()


def body(right_side, kappa_squared, hdiff, obs_weight):
    wide = pltpu.VMEM((EX, ET, NA), jnp.float32)
    block = pltpu.VMEM((NX, NT, NA), jnp.float32)
    most = max(len(list(itertools.product(*[range(SIZES[a]) for a in axes]))) for axes in STAGES)
    dma = pltpu.SemaphoreType.DMA
    return pl.pallas_call(
        solve_kernel,
        out_shape=(jax.ShapeDtypeStruct((NX, NT, NA), jnp.float32),) * 2,
        in_specs=[pl.BlockSpec(memory_space=pl.ANY)] * 4,
        out_specs=(pl.BlockSpec(memory_space=pltpu.VMEM),) * 2,
        scratch_shapes=[wide] * 14 + [block] + [wide] + [block]
        + [pltpu.VMEM((8, 128), jnp.float32), pltpu.VMEM((len(STAGES), most, 128), jnp.float32)]
        + [dma((4,)), dma((6, 2)), dma((6, 2)), dma((9, 2)), dma((9, 2)), dma((5, 4)), dma((5, 4)),
           dma((len(STAGES), most)), dma((len(STAGES), most))],
        compiler_params=pltpu.CompilerParams(
            collective_id=0, has_side_effects=True, vmem_limit_bytes=62 * 2**20
        ),
    )(right_side, kappa_squared, hdiff, obs_weight)


def solution(mesh):
    placed = P("lon", "tm", None)
    return jax.shard_map(
        body, mesh=mesh, in_specs=(placed,) * 4, out_specs=(placed,) * 2, check_vma=False
    )
```

```python
import itertools

import jax
import jax.numpy as jnp
from jax import lax
from jax.experimental import pallas as pl
from jax.experimental.pallas import tpu as pltpu
from jax.sharding import PartitionSpec as P

MESH = pl.DeviceIdType.MESH
SIZES = {"x": 4, "z": 12, "h": 2, "c": 2, "l": 4}
PLANES = 2
REST = 12 - PLANES
BUDGET = 107 * 2**19
NX, NT, NA = 8, 24, 256
HX, HT = 3, 8
EX, ET = NX + 2 * HX, NT + 2 * HT
T0, T1 = HT, HT + NT


def place():
    lon, tm = lax.axis_index("lon"), lax.axis_index("tm")
    return {"c": lon % 2, "h": (lon // 2) % 2, "z": (lon // 4) % 12, "x": lon // 48, "l": tm}


def peers(axes):
    here, out = place(), []
    lon, tm = lax.axis_index("lon"), lax.axis_index("tm")
    steps = {"x": 48, "z": 4, "h": 2, "c": 1}

    def moves(axis):
        at, size, step = here[axis], SIZES[axis], steps.get(axis, 1)
        return [0] + [step * (i - size * (at + i >= size).astype(jnp.int32)) for i in range(1, size)]

    shifts = {a: moves(a) for a in axes}
    for offset in itertools.product(*[range(SIZES[a]) for a in axes]):
        if any(offset):
            to_lon, to_tm = lon, tm
            for a, i in zip(axes, offset):
                if i and a == "l":
                    to_tm = to_tm + shifts[a][i]
                elif i:
                    to_lon = to_lon + shifts[a][i]
            out.append((to_lon, to_tm))
    return out


def face(here, there):
    total = here + there
    return jnp.where(total > 0, 2.0 * here * there / jnp.where(total > 0, total, 1.0), 0.0)


def roll(v, step, axis):
    return pltpu.roll(v, step % v.shape[axis], axis)


def solve_kernel(b_in, k_in, h_in, o_in, x_out, r_out,
                 b, k, h, o, fx, ft, fl, d, m, y0, y1, y2, u, v, w1, w2, w3, early, late, outer, row, gathered, slots, total,
                 in_sem, s_tm, r_tm, s_lon, r_lon, s_cor, r_cor,
                 s_gather, r_gather, s_plane, r_plane, s_total, r_total):
    lon, tm = lax.axis_index("lon"), lax.axis_index("tm")
    east, west = lax.rem(lon + 1, 192), lax.rem(lon + 191, 192)
    up, down = lax.rem(tm + 1, 4), lax.rem(tm + 3, 4)

    barrier = pltpu.get_barrier_semaphore()
    near = [(east, tm), (west, tm), (lon, up), (lon, down), (east, up), (east, down), (west, up), (west, down)]
    for who in near:
        pl.semaphore_signal(barrier, inc=1, device_id=who, device_id_type=MESH)

    mine = [
        pltpu.make_async_copy(src, dst.at[pl.ds(HX, NX), pl.ds(T0, NT)], in_sem.at[i])
        for i, (src, dst) in enumerate(((b_in, b), (k_in, k), (h_in, h), (o_in, o)))
    ]
    for copy in mine:
        copy.start()

    here = place()
    z, core = here["z"], here["c"]
    collects = z < PLANES
    column0 = lon - z * 4 - core
    plane = peers(("x", "h", "l"))

    def column(at_z, at_core):
        return (column0 + at_z * 4 + at_core, tm)

    heard_from = jnp.where(z < PLANES + REST // 2, 1, 0)
    spread = [jnp.where(z == 0, PLANES + REST // 2 + i, PLANES + i) for i in range(REST // 2)]

    @pl.when(collects)
    def _():
        for who in plane + peers(("z", "c")):
            pl.semaphore_signal(barrier, inc=1, device_id=who, device_id_type=MESH)

    @pl.when(jnp.logical_not(collects))
    def _():
        pl.semaphore_signal(barrier, inc=1, device_id=column(heard_from, core), device_id_type=MESH)

    edges = ((h, 0.0), (k, 1.0), (o, 1.0), (b, 0.0), (y1, 0.0), (v, 0.0))

    @pl.when(tm == 0)
    def _():
        for ref, value in edges:
            ref[:, :T0] = jnp.full((EX, HT, NA), value, jnp.float32)

    @pl.when(tm == 3)
    def _():
        for ref, value in edges:
            ref[:, T1:] = jnp.full((EX, HT, NA), value, jnp.float32)

    lat_own = lax.broadcasted_iota(jnp.int32, (NT, NA), 1)

    def own_y0(s):
        at = h[s, T0:T1]
        ftv = face(at, roll(at, -1, 0))
        flv = jnp.where(lat_own == NA - 1, 0.0, face(at, roll(at, -1, 1)))
        around = (face(at, h[s + 1, T0:T1]), face(h[s - 1, T0:T1], at), ftv, roll(ftv, 1, 0), flv, roll(flv, 1, 1))
        total, squares = k[s, T0:T1], o[s, T0:T1]
        for f in around:
            total += f
            squares += f * f
        return b[s, T0:T1] / (total * total + squares)

    for copy in mine:
        copy.wait()
    early[0] = own_y0(HX + NX - 2)
    early[1] = own_y0(HX + 1)

    @pl.when(collects)
    def _():
        pl.semaphore_wait(barrier, len(near) + 2 * PLANES - 1 + len(plane) + REST // 2)

    @pl.when(jnp.logical_not(collects))
    def _():
        pl.semaphore_wait(barrier, len(near) + 2 * PLANES)

    def remote(src, dst, ssem, rsem, who):
        return pltpu.make_async_remote_copy(src, dst, ssem, rsem, device_id=who, device_id_type=MESH)

    class Lon:
        def __init__(self, n, src, off_x, off_t, dst, depth, width=1):
            def part(at):
                return src.at[pl.ds(off_x + at, width), pl.ds(off_t, NT)]

            def halo(at):
                return dst.at[pl.ds(at, width), pl.ds(T0, NT)]

            self.copies = [
                remote(part(NX - depth - width + 1), halo(HX - depth - width + 1),
                       s_lon.at[n, 0], r_lon.at[n, 0], (east, tm)),
                remote(part(depth - 1), halo(HX + NX + depth - 1),
                       s_lon.at[n, 1], r_lon.at[n, 1], (west, tm)),
            ]

        def start(self):
            for copy in self.copies:
                copy.start()

        def received(self):
            for copy in self.copies:
                copy.wait_recv()

        def sent(self):
            for copy in self.copies:
                copy.wait_send()

    class Tm:
        def __init__(self, upward, downward):
            self.upward, self.downward = upward, downward

        def run(self, what, towards, back):
            @pl.when(towards)
            def _():
                for copy in self.upward:
                    getattr(copy, what)()

            @pl.when(back)
            def _():
                for copy in self.downward:
                    getattr(copy, what)()

        def start(self):
            self.run("start", tm < 3, tm > 0)

        def received(self):
            self.run("wait_recv", tm > 0, tm < 3)

        def sent(self):
            self.run("wait_send", tm < 3, tm > 0)

    def rows(n, src, off_x, off_t, dst, width):
        return Tm(
            [remote(src.at[pl.ds(off_x, NX), pl.ds(off_t + NT - width, width)],
                    dst.at[pl.ds(HX, NX), pl.ds(T0 - width, width)], s_tm.at[n, 0], r_tm.at[n, 0], (lon, up))],
            [remote(src.at[pl.ds(off_x, NX), pl.ds(off_t, width)],
                    dst.at[pl.ds(HX, NX), pl.ds(T1, width)], s_tm.at[n, 1], r_tm.at[n, 1], (lon, down))],
        )

    def corners(n, src, off_x, off_t, dst, width):
        def make(i, sx, st, dx, dt, who):
            return remote(src.at[pl.ds(off_x + sx, width), pl.ds(off_t + st, width)],
                          dst.at[pl.ds(dx, width), pl.ds(dt, width)], s_cor.at[n, i], r_cor.at[n, i], who)

        return Tm(
            [make(0, NX - width, NT - width, HX - width, T0 - width, (east, up)),
             make(1, 0, NT - width, HX + NX, T0 - width, (west, up))],
            [make(2, NX - width, 0, HX - width, T1, (east, down)),
             make(3, 0, 0, HX + NX, T1, (west, down))],
        )

    inputs = ((h_in, h), (k_in, k), (o_in, o), (b_in, b))
    tm_first = [rows(i, src, 0, 0, dst, 3 if i == 0 else 2) for i, (src, dst) in enumerate(inputs)]
    lon_first = [Lon(i, src, 0, 0, dst, 1, 2 if i == 0 else 1) for i, (src, dst) in enumerate(inputs)]
    cor_first = [corners(i, src, 0, 0, dst, 2 if i == 0 else 1) for i, (src, dst) in enumerate(inputs)]
    class Pair(Lon):
        def __init__(self, n, eastward, westward):
            self.copies = [
                remote(*eastward, s_lon.at[n, 0], r_lon.at[n, 0], (east, tm)),
                remote(*westward, s_lon.at[n, 1], r_lon.at[n, 1], (west, tm)),
            ]

    lon_y0 = Pair(4, (early.at[0], late.at[0]), (early.at[1], late.at[1]))
    low, high = pl.ds(T0, 1), pl.ds(T1 - 1, 1)
    inner = (pl.ds(HX + NX - 2, 1), pl.ds(HX + 1, 1))
    lon_rows = [
        Pair(9, (y0.at[inner[0], low], outer.at[pl.ds(0, 1), pl.ds(0, 1)]),
             (y0.at[inner[1], low], outer.at[pl.ds(1, 1), pl.ds(0, 1)])),
        Pair(10, (y0.at[inner[0], high], outer.at[pl.ds(0, 1), pl.ds(7, 1)]),
             (y0.at[inner[1], high], outer.at[pl.ds(1, 1), pl.ds(7, 1)])),
    ]
    lon_late = [Lon(5, h_in, 0, 0, h, 3), Lon(6, k_in, 0, 0, k, 2)]

    tm_first[0].start()
    lon_first[0].start()
    for i in (1, 2, 3):
        tm_first[i].start()
    for i in (1, 2, 3):
        lon_first[i].start()
    lon_y0.start()
    for copies in cor_first:
        copies.start()

    lat = lax.broadcasted_iota(jnp.int32, (ET, NA), 1)

    def stencil(field, s):
        here = field[s]
        ftv, flv = ft[s], fl[s]
        sides = fx[s] * field[s + 1] + fx[s - 1] * field[s - 1]
        sides += ftv * roll(here, -1, 0) + roll(ftv * here, 1, 0)
        sides += flv * roll(here, -1, 1) + roll(flv * here, 1, 1)
        return d[s] * here - sides

    def across(*slabs):
        for s in slabs:
            fx[s] = face(h[s], h[s + 1])

    def within(*slabs):
        for s in slabs:
            here = h[s]
            ft[s] = face(here, roll(here, -1, 0))
            fl[s] = jnp.where(lat == NA - 1, 0.0, face(here, roll(here, -1, 1)))

    def diagonal(*slabs, full=True):
        for s in slabs:
            ftv, flv = ft[s], fl[s]
            around = (fx[s], fx[s - 1], ftv, roll(ftv, 1, 0), flv, roll(flv, 1, 1))
            total = k[s]
            for f in around:
                total += f
            d[s] = total
            if full:
                squares = o[s]
                for f in around:
                    squares += f * f
                inverse = 1.0 / (total * total + squares)
                m[s] = inverse
                y0[s] = inverse * b[s]

    def apply(src, *slabs):
        for s in slabs:
            u[s] = stencil(src, s)

    def next_first(*slabs):
        for s in slabs:
            w = (stencil(u, s) + o[s] * y0[s])[T0:T1]
            w1[s - HX] = w
            y1[s, T0:T1] = m[s, T0:T1] * w

    def next_second(*slabs):
        for s in slabs:
            w = stencil(u, s) + o[s] * y1[s]
            w2[s] = w
            y2[s] = m[s] * w

    for copies in tm_first:
        copies.received()
    across(3, 4, 8, 9)
    within(4, 9)
    diagonal(4, 9)
    for copies in lon_rows + lon_late:
        copies.start()
    across(5, 6, 7)
    within(3, 5, 6, 7, 8, 10)
    diagonal(5, 6, 7, 8)
    apply(y0, 5, 6, 7, 8)
    next_first(6, 7)

    lon_first[0].received()
    cor_first[0].received()
    across(1, 2, 10, 11)
    within(2, 11)
    diagonal(3, 10)
    apply(y0, 4, 9)
    next_first(5, 8)
    for i in (1, 2, 3):
        lon_first[i].received()
        cor_first[i].received()
    diagonal(2, 11)
    apply(y0, 3, 10)
    next_first(4, 9)
    for copies in [lon_y0] + lon_rows:
        copies.received()
    step = lax.broadcasted_iota(jnp.int32, (NT, NA), 0)
    for side, s in enumerate((1, EX - 2)):
        layer = jnp.where(step == 0, outer[side, 0:1], late[side])
        y0[s, T0:T1] = jnp.where(step == NT - 1, outer[side, 7:8], layer)
    apply(y0, 2, 11)
    next_first(3, 10)

    lon_y1 = Lon(7, y1, HX, T0, y1, 1, 3)
    tm_y1 = rows(4, y1, HX, T0, y1, 3)
    cor_y1 = corners(4, y1, HX, T0, y1, 2)
    lon_y1.start()
    tm_y1.start()
    cor_y1.start()

    for copies in lon_late:
        copies.received()
    across(0, 12)
    within(1, 12)
    diagonal(1, 12, full=False)
    tm_y1.received()
    apply(y1, 4, 5, 6, 7, 8, 9)
    next_second(5, 6, 7, 8)

    sums = [jnp.zeros((NT, NA), jnp.float32)] * 6

    def moments(*slabs):
        for s in slabs:
            t = stencil(y2, s)[T0:T1]
            v[s, T0:T1] = t
            yy0, yy1, yy2 = y0[s, T0:T1], y1[s, T0:T1], y2[s, T0:T1]
            ww1, ww2 = w1[s - HX], w2[s, T0:T1]
            terms = (b[s, T0:T1] * yy0, yy0 * ww1, ww1 * yy1, ww1 * yy2, ww2 * yy2,
                     t * t + o[s, T0:T1] * yy2 * yy2)
            for i, term in enumerate(terms):
                sums[i] = sums[i] + term

    moments(6, 7)
    lon_y1.received()
    cor_y1.received()
    apply(y1, 1, 2, 3, 10, 11, 12)
    next_second(2, 3, 4, 9, 10, 11)
    moments(3, 4, 5, 8, 9, 10)

    lane = lax.broadcasted_iota(jnp.int32, (1, 128), 1)
    packed = jnp.zeros((1, 128), jnp.float32)
    for i, part in enumerate(sums):
        packed = jnp.where(lane == i, jnp.sum(part, keepdims=True), packed)

    lon_u2 = Lon(8, v, HX, T0, v, 1)
    tm_u2 = rows(5, v, HX, T0, v, 1)
    row[pl.ds(0, 1)] = packed
    targets = [(at_z, at_core) for at_z in range(PLANES) for at_core in range(2)]
    gather = []
    for i, (at_z, at_core) in enumerate(targets):
        back = z - at_z + 12 * (z < at_z).astype(jnp.int32)
        slot = back * 2 + jnp.where(core == at_core, 0, 1)
        gather.append((slot != 0, remote(
            row.at[pl.ds(0, 1)], gathered.at[slot], s_gather.at[i], r_gather.at[slot], column(at_z, at_core))))
    for other, copy in gather:
        @pl.when(other)
        def _():
            copy.start()

    lon_u2.start()
    tm_u2.start()

    exchange = [
        remote(row.at[pl.ds(1, 1)], slots.at[pl.ds(i, 1)], s_plane.at[i], r_plane.at[i], who)
        for i, who in enumerate(plane)
    ]
    total_out = [
        remote(total, total, s_total.at[i], r_total.at[0], column(at_z, core)) for i, at_z in enumerate(spread)
    ]

    @pl.when(collects)
    def _():
        value = row[pl.ds(0, 1)]
        for i in range(1, 24):
            remote(row.at[pl.ds(0, 1)], gathered.at[i], s_gather.at[0], r_gather.at[i], (east, tm)).wait_recv()
            value = value + gathered[i]
        row[pl.ds(1, 1)] = value
        for copy in exchange:
            copy.start()

    tm_u2.received()
    lon_u2.received()
    for s in range(HX, HX + NX):
        w3[s - HX] = (stencil(v, s) + o[s] * y2[s])[T0:T1]

    @pl.when(collects)
    def _():
        for copy in exchange:
            copy.wait_recv()
        total[...] = row[pl.ds(1, 1)] + jnp.sum(slots[: len(plane)], axis=0, keepdims=True)
        for copy in total_out:
            copy.start()

    @pl.when(jnp.logical_not(collects))
    def _():
        total_out[0].wait_recv()

    packed = total[...]
    mu = [packed[:, i : i + 1] for i in range(6)]

    def form(c, shift):
        total = 0.0
        for i, a in enumerate(c):
            for j, e in enumerate(c):
                total = total + a * e * mu[i + j + shift]
        return total

    a0 = mu[0] / mu[1]
    rho1 = [jnp.ones_like(a0), -a0]
    rz1 = form(rho1, 0)
    beta0 = rz1 / mu[0]
    p1 = [1.0 + beta0, -a0]
    a1 = rz1 / form(p1, 1)
    rho2 = [jnp.ones_like(a0), -a0 - a1 * p1[0], -a1 * p1[1]]
    rz2 = form(rho2, 0)
    beta1 = rz2 / rz1
    p2 = [rho2[0] + beta1 * p1[0], rho2[1] + beta1 * p1[1], rho2[2]]
    a2 = rz2 / form(p2, 1)
    c = (a0 + a1 * p1[0] + a2 * p2[0], a1 * p1[1] + a2 * p2[1], a2 * p2[2])
    c0, c1, c2 = (jnp.broadcast_to(value, (NT, NA)) for value in c)
    for s in range(NX):
        e = s + HX
        x_out[s] = c0 * y0[e, T0:T1] + c1 * y1[e, T0:T1] + c2 * y2[e, T0:T1]
        r_out[s] = b[e, T0:T1] - (c0 * w1[s] + c1 * w2[e, T0:T1] + c2 * w3[s])

    for copies in tm_first + lon_first + cor_first + lon_late + lon_rows + [lon_y0, lon_y1, tm_y1, cor_y1, lon_u2, tm_u2]:
        copies.sent()
    for other, copy in gather:
        @pl.when(other)
        def _():
            copy.wait_send()

    @pl.when(collects)
    def _():
        for copy in exchange + total_out:
            copy.wait_send()


def body(right_side, kappa_squared, hdiff, obs_weight):
    wide = pltpu.VMEM((EX, ET, NA), jnp.float32)
    block = pltpu.VMEM((NX, NT, NA), jnp.float32)
    dma = pltpu.SemaphoreType.DMA
    return pl.pallas_call(
        solve_kernel,
        out_shape=(jax.ShapeDtypeStruct((NX, NT, NA), jnp.float32),) * 2,
        in_specs=[pl.BlockSpec(memory_space=pl.ANY)] * 4,
        out_specs=(pl.BlockSpec(memory_space=pltpu.VMEM),) * 2,
        scratch_shapes=[wide] * 14 + [block] + [wide] + [block]
        + [pltpu.VMEM(shape, jnp.float32) for shape in (
            (2, NT, NA), (2, NT, NA), (2, 8, NA), (8, 128), (24, 1, 128), (32, 128), (1, 128))]
        + [dma((4,)), dma((6, 2)), dma((6, 2)), dma((11, 2)), dma((11, 2)), dma((5, 4)), dma((5, 4)),
           dma((4,)), dma((24,)), dma((32,)), dma((32,)), dma((REST // 2,)), dma((1,))],
        compiler_params=pltpu.CompilerParams(
            collective_id=0, has_side_effects=True, vmem_limit_bytes=BUDGET
        ),
    )(right_side, kappa_squared, hdiff, obs_weight)


def solution(mesh):
    placed = P("lon", "tm", None)
    return jax.shard_map(
        body, mesh=mesh, in_specs=(placed,) * 4, out_specs=(placed,) * 2, check_vma=False
    )
```

```python
import itertools

import jax
import jax.numpy as jnp
from jax import lax
from jax.experimental import pallas as pl
from jax.experimental.pallas import tpu as pltpu
from jax.sharding import PartitionSpec as P

MESH = pl.DeviceIdType.MESH
SIZES = {"x": 4, "z": 12, "h": 2, "c": 2, "l": 4}
PLANES = 3
REST = 12 - PLANES
BUDGET = 107 * 2**19
NX, NT, NA = 8, 24, 256
HX, HT = 3, 8
EX, ET = NX + 2 * HX, NT + 2 * HT
T0, T1 = HT, HT + NT


def place():
    lon, tm = lax.axis_index("lon"), lax.axis_index("tm")
    return {"c": lon % 2, "h": (lon // 2) % 2, "z": (lon // 4) % 12, "x": lon // 48, "l": tm}


def peers(axes):
    here, out = place(), []
    lon, tm = lax.axis_index("lon"), lax.axis_index("tm")
    steps = {"x": 48, "z": 4, "h": 2, "c": 1}

    def moves(axis):
        at, size, step = here[axis], SIZES[axis], steps.get(axis, 1)
        return [0] + [step * (i - size * (at + i >= size).astype(jnp.int32)) for i in range(1, size)]

    shifts = {a: moves(a) for a in axes}
    for offset in itertools.product(*[range(SIZES[a]) for a in axes]):
        if any(offset):
            to_lon, to_tm = lon, tm
            for a, i in zip(axes, offset):
                if i and a == "l":
                    to_tm = to_tm + shifts[a][i]
                elif i:
                    to_lon = to_lon + shifts[a][i]
            out.append((to_lon, to_tm))
    return out


def face(here, there):
    total = here + there
    return jnp.where(total > 0, 2.0 * here * there / jnp.where(total > 0, total, 1.0), 0.0)


def roll(v, step, axis):
    return pltpu.roll(v, step % v.shape[axis], axis)


def solve_kernel(b_in, k_in, h_in, o_in, x_out, r_out,
                 b, k, h, o, fx, ft, fl, d, m, y0, y1, y2, u, v, w1, w2, w3, early, late, outer, row, gathered, slots, total,
                 in_sem, s_tm, r_tm, s_lon, r_lon, s_cor, r_cor,
                 s_gather, r_gather, s_plane, r_plane, s_total, r_total):
    lon, tm = lax.axis_index("lon"), lax.axis_index("tm")
    east, west = lax.rem(lon + 1, 192), lax.rem(lon + 191, 192)
    up, down = lax.rem(tm + 1, 4), lax.rem(tm + 3, 4)

    barrier = pltpu.get_barrier_semaphore()
    near = [(east, tm), (west, tm), (lon, up), (lon, down), (east, up), (east, down), (west, up), (west, down)]
    for who in near:
        pl.semaphore_signal(barrier, inc=1, device_id=who, device_id_type=MESH)

    mine = [
        pltpu.make_async_copy(src, dst.at[pl.ds(HX, NX), pl.ds(T0, NT)], in_sem.at[i])
        for i, (src, dst) in enumerate(((b_in, b), (k_in, k), (h_in, h), (o_in, o)))
    ]
    for copy in mine:
        copy.start()

    here = place()
    z, core = here["z"], here["c"]
    collects = z < PLANES
    column0 = lon - z * 4 - core
    plane = peers(("x", "h", "l"))

    def column(at_z, at_core):
        return (column0 + at_z * 4 + at_core, tm)

    spreads = z == PLANES - 1
    spread = [PLANES + i for i in range(REST)]

    @pl.when(collects)
    def _():
        for who in plane + peers(("z", "c")):
            pl.semaphore_signal(barrier, inc=1, device_id=who, device_id_type=MESH)

    @pl.when(jnp.logical_not(collects))
    def _():
        pl.semaphore_signal(barrier, inc=1, device_id=column(PLANES - 1, core), device_id_type=MESH)

    edges = ((h, 0.0), (k, 1.0), (o, 1.0), (b, 0.0), (y1, 0.0), (v, 0.0))

    @pl.when(tm == 0)
    def _():
        for ref, value in edges:
            ref[:, :T0] = jnp.full((EX, HT, NA), value, jnp.float32)

    @pl.when(tm == 3)
    def _():
        for ref, value in edges:
            ref[:, T1:] = jnp.full((EX, HT, NA), value, jnp.float32)

    lat_own = lax.broadcasted_iota(jnp.int32, (NT, NA), 1)

    def own_y0(s):
        at = h[s, T0:T1]
        ftv = face(at, roll(at, -1, 0))
        flv = jnp.where(lat_own == NA - 1, 0.0, face(at, roll(at, -1, 1)))
        around = (face(at, h[s + 1, T0:T1]), face(h[s - 1, T0:T1], at), ftv, roll(ftv, 1, 0), flv, roll(flv, 1, 1))
        total, squares = k[s, T0:T1], o[s, T0:T1]
        for f in around:
            total += f
            squares += f * f
        return b[s, T0:T1] / (total * total + squares)

    for copy in mine:
        copy.wait()
    early[0] = own_y0(HX + NX - 2)
    early[1] = own_y0(HX + 1)

    @pl.when(collects)
    def _():
        pl.semaphore_wait(barrier, len(near) + 2 * PLANES - 1 + len(plane) + jnp.where(spreads, REST, 0))

    @pl.when(jnp.logical_not(collects))
    def _():
        pl.semaphore_wait(barrier, len(near) + 2 * PLANES)

    def remote(src, dst, ssem, rsem, who):
        return pltpu.make_async_remote_copy(src, dst, ssem, rsem, device_id=who, device_id_type=MESH)

    class Lon:
        def __init__(self, n, src, off_x, off_t, dst, depth, width=1):
            def part(at):
                return src.at[pl.ds(off_x + at, width), pl.ds(off_t, NT)]

            def halo(at):
                return dst.at[pl.ds(at, width), pl.ds(T0, NT)]

            self.copies = [
                remote(part(NX - depth - width + 1), halo(HX - depth - width + 1),
                       s_lon.at[n, 0], r_lon.at[n, 0], (east, tm)),
                remote(part(depth - 1), halo(HX + NX + depth - 1),
                       s_lon.at[n, 1], r_lon.at[n, 1], (west, tm)),
            ]

        def start(self):
            for copy in self.copies:
                copy.start()

        def received(self):
            for copy in self.copies:
                copy.wait_recv()

        def sent(self):
            for copy in self.copies:
                copy.wait_send()

    class Tm:
        def __init__(self, upward, downward):
            self.upward, self.downward = upward, downward

        def run(self, what, towards, back):
            @pl.when(towards)
            def _():
                for copy in self.upward:
                    getattr(copy, what)()

            @pl.when(back)
            def _():
                for copy in self.downward:
                    getattr(copy, what)()

        def start(self):
            self.run("start", tm < 3, tm > 0)

        def received(self):
            self.run("wait_recv", tm > 0, tm < 3)

        def sent(self):
            self.run("wait_send", tm < 3, tm > 0)

    def rows(n, src, off_x, off_t, dst, width):
        return Tm(
            [remote(src.at[pl.ds(off_x, NX), pl.ds(off_t + NT - width, width)],
                    dst.at[pl.ds(HX, NX), pl.ds(T0 - width, width)], s_tm.at[n, 0], r_tm.at[n, 0], (lon, up))],
            [remote(src.at[pl.ds(off_x, NX), pl.ds(off_t, width)],
                    dst.at[pl.ds(HX, NX), pl.ds(T1, width)], s_tm.at[n, 1], r_tm.at[n, 1], (lon, down))],
        )

    def corners(n, src, off_x, off_t, dst, width):
        def make(i, sx, st, dx, dt, who):
            return remote(src.at[pl.ds(off_x + sx, width), pl.ds(off_t + st, width)],
                          dst.at[pl.ds(dx, width), pl.ds(dt, width)], s_cor.at[n, i], r_cor.at[n, i], who)

        return Tm(
            [make(0, NX - width, NT - width, HX - width, T0 - width, (east, up)),
             make(1, 0, NT - width, HX + NX, T0 - width, (west, up))],
            [make(2, NX - width, 0, HX - width, T1, (east, down)),
             make(3, 0, 0, HX + NX, T1, (west, down))],
        )

    inputs = ((h_in, h), (k_in, k), (o_in, o), (b_in, b))
    tm_first = [rows(i, src, 0, 0, dst, 3 if i == 0 else 2) for i, (src, dst) in enumerate(inputs)]
    lon_first = [Lon(i, src, 0, 0, dst, 1, 2 if i == 0 else 1) for i, (src, dst) in enumerate(inputs)]
    cor_first = [corners(i, src, 0, 0, dst, 2 if i == 0 else 1) for i, (src, dst) in enumerate(inputs)]
    class Pair(Lon):
        def __init__(self, n, eastward, westward):
            self.copies = [
                remote(*eastward, s_lon.at[n, 0], r_lon.at[n, 0], (east, tm)),
                remote(*westward, s_lon.at[n, 1], r_lon.at[n, 1], (west, tm)),
            ]

    lon_y0 = Pair(4, (early.at[0], late.at[0]), (early.at[1], late.at[1]))
    low, high = pl.ds(T0, 1), pl.ds(T1 - 1, 1)
    inner = (pl.ds(HX + NX - 2, 1), pl.ds(HX + 1, 1))
    lon_rows = [
        Pair(9, (y0.at[inner[0], low], outer.at[pl.ds(0, 1), pl.ds(0, 1)]),
             (y0.at[inner[1], low], outer.at[pl.ds(1, 1), pl.ds(0, 1)])),
        Pair(10, (y0.at[inner[0], high], outer.at[pl.ds(0, 1), pl.ds(7, 1)]),
             (y0.at[inner[1], high], outer.at[pl.ds(1, 1), pl.ds(7, 1)])),
    ]
    lon_late = [Lon(5, h_in, 0, 0, h, 3), Lon(6, k_in, 0, 0, k, 2)]

    tm_first[0].start()
    lon_first[0].start()
    for i in (1, 2, 3):
        tm_first[i].start()
    for i in (1, 2, 3):
        lon_first[i].start()
    lon_y0.start()
    for copies in cor_first:
        copies.start()

    lat = lax.broadcasted_iota(jnp.int32, (ET, NA), 1)

    def stencil(field, s):
        here = field[s]
        ftv, flv = ft[s], fl[s]
        sides = fx[s] * field[s + 1] + fx[s - 1] * field[s - 1]
        sides += ftv * roll(here, -1, 0) + roll(ftv * here, 1, 0)
        sides += flv * roll(here, -1, 1) + roll(flv * here, 1, 1)
        return d[s] * here - sides

    def across(*slabs):
        for s in slabs:
            fx[s] = face(h[s], h[s + 1])

    def within(*slabs):
        for s in slabs:
            here = h[s]
            ft[s] = face(here, roll(here, -1, 0))
            fl[s] = jnp.where(lat == NA - 1, 0.0, face(here, roll(here, -1, 1)))

    def diagonal(*slabs, full=True):
        for s in slabs:
            ftv, flv = ft[s], fl[s]
            around = (fx[s], fx[s - 1], ftv, roll(ftv, 1, 0), flv, roll(flv, 1, 1))
            total = k[s]
            for f in around:
                total += f
            d[s] = total
            if full:
                squares = o[s]
                for f in around:
                    squares += f * f
                inverse = 1.0 / (total * total + squares)
                m[s] = inverse
                y0[s] = inverse * b[s]

    def apply(src, *slabs):
        for s in slabs:
            u[s] = stencil(src, s)

    def next_first(*slabs):
        for s in slabs:
            w = (stencil(u, s) + o[s] * y0[s])[T0:T1]
            w1[s - HX] = w
            y1[s, T0:T1] = m[s, T0:T1] * w

    def next_second(*slabs):
        for s in slabs:
            w = stencil(u, s) + o[s] * y1[s]
            w2[s] = w
            y2[s] = m[s] * w

    for copies in tm_first:
        copies.received()
    across(3, 4, 8, 9)
    within(4, 9)
    diagonal(4, 9)
    for copies in lon_rows + lon_late:
        copies.start()
    across(5, 6, 7)
    within(3, 5, 6, 7, 8, 10)
    diagonal(5, 6, 7, 8)
    apply(y0, 5, 6, 7, 8)
    next_first(6, 7)

    lon_first[0].received()
    cor_first[0].received()
    across(1, 2, 10, 11)
    within(2, 11)
    diagonal(3, 10)
    apply(y0, 4, 9)
    next_first(5, 8)
    for i in (1, 2, 3):
        lon_first[i].received()
        cor_first[i].received()
    diagonal(2, 11)
    apply(y0, 3, 10)
    next_first(4, 9)
    for copies in [lon_y0] + lon_rows:
        copies.received()
    step = lax.broadcasted_iota(jnp.int32, (NT, NA), 0)
    for side, s in enumerate((1, EX - 2)):
        layer = jnp.where(step == 0, outer[side, 0:1], late[side])
        y0[s, T0:T1] = jnp.where(step == NT - 1, outer[side, 7:8], layer)
    apply(y0, 2, 11)
    next_first(3, 10)

    lon_y1 = Lon(7, y1, HX, T0, y1, 1, 3)
    tm_y1 = rows(4, y1, HX, T0, y1, 3)
    cor_y1 = corners(4, y1, HX, T0, y1, 2)
    lon_y1.start()
    tm_y1.start()
    cor_y1.start()

    for copies in lon_late:
        copies.received()
    across(0, 12)
    within(1, 12)
    diagonal(1, 12, full=False)
    tm_y1.received()
    apply(y1, 4, 5, 6, 7, 8, 9)
    next_second(5, 6, 7, 8)

    sums = [jnp.zeros((NT, NA), jnp.float32)] * 6

    def moments(*slabs):
        for s in slabs:
            t = stencil(y2, s)[T0:T1]
            v[s, T0:T1] = t
            yy0, yy1, yy2 = y0[s, T0:T1], y1[s, T0:T1], y2[s, T0:T1]
            ww1, ww2 = w1[s - HX], w2[s, T0:T1]
            terms = (b[s, T0:T1] * yy0, yy0 * ww1, ww1 * yy1, ww1 * yy2, ww2 * yy2,
                     t * t + o[s, T0:T1] * yy2 * yy2)
            for i, term in enumerate(terms):
                sums[i] = sums[i] + term

    moments(6, 7)
    lon_y1.received()
    cor_y1.received()
    apply(y1, 1, 2, 3, 10, 11, 12)
    next_second(2, 3, 4, 9, 10, 11)
    moments(3, 4, 5, 8, 9, 10)

    lane = lax.broadcasted_iota(jnp.int32, (1, 128), 1)
    packed = jnp.zeros((1, 128), jnp.float32)
    for i, part in enumerate(sums):
        packed = jnp.where(lane == i, jnp.sum(part, keepdims=True), packed)

    lon_u2 = Lon(8, v, HX, T0, v, 1)
    tm_u2 = rows(5, v, HX, T0, v, 1)
    row[pl.ds(0, 1)] = packed
    targets = [(at_z, at_core) for at_z in range(PLANES) for at_core in range(2)]
    gather = []
    for i, (at_z, at_core) in enumerate(targets):
        back = z - at_z + 12 * (z < at_z).astype(jnp.int32)
        slot = back * 2 + jnp.where(core == at_core, 0, 1)
        gather.append((slot != 0, remote(
            row.at[pl.ds(0, 1)], gathered.at[slot], s_gather.at[i], r_gather.at[slot], column(at_z, at_core))))
    for other, copy in gather:
        @pl.when(other)
        def _():
            copy.start()

    lon_u2.start()
    tm_u2.start()

    exchange = [
        remote(row.at[pl.ds(1, 1)], slots.at[pl.ds(i, 1)], s_plane.at[i], r_plane.at[i], who)
        for i, who in enumerate(plane)
    ]
    total_out = [
        remote(total, total, s_total.at[i], r_total.at[0], column(at_z, core)) for i, at_z in enumerate(spread)
    ]

    @pl.when(collects)
    def _():
        value = row[pl.ds(0, 1)]
        for i in range(1, 24):
            remote(row.at[pl.ds(0, 1)], gathered.at[i], s_gather.at[0], r_gather.at[i], (east, tm)).wait_recv()
            value = value + gathered[i]
        row[pl.ds(1, 1)] = value
        for copy in exchange:
            copy.start()

    tm_u2.received()
    lon_u2.received()
    for s in range(HX, HX + NX):
        w3[s - HX] = (stencil(v, s) + o[s] * y2[s])[T0:T1]

    @pl.when(collects)
    def _():
        for copy in exchange:
            copy.wait_recv()
        total[...] = row[pl.ds(1, 1)] + jnp.sum(slots[: len(plane)], axis=0, keepdims=True)

        @pl.when(spreads)
        def _():
            for copy in total_out:
                copy.start()

    @pl.when(jnp.logical_not(collects))
    def _():
        total_out[0].wait_recv()

    packed = total[...]
    mu = [packed[:, i : i + 1] for i in range(6)]

    def form(c, shift):
        total = 0.0
        for i, a in enumerate(c):
            for j, e in enumerate(c):
                total = total + a * e * mu[i + j + shift]
        return total

    a0 = mu[0] / mu[1]
    rho1 = [jnp.ones_like(a0), -a0]
    rz1 = form(rho1, 0)
    beta0 = rz1 / mu[0]
    p1 = [1.0 + beta0, -a0]
    a1 = rz1 / form(p1, 1)
    rho2 = [jnp.ones_like(a0), -a0 - a1 * p1[0], -a1 * p1[1]]
    rz2 = form(rho2, 0)
    beta1 = rz2 / rz1
    p2 = [rho2[0] + beta1 * p1[0], rho2[1] + beta1 * p1[1], rho2[2]]
    a2 = rz2 / form(p2, 1)
    c = (a0 + a1 * p1[0] + a2 * p2[0], a1 * p1[1] + a2 * p2[1], a2 * p2[2])
    c0, c1, c2 = (jnp.broadcast_to(value, (NT, NA)) for value in c)
    for s in range(NX):
        e = s + HX
        x_out[s] = c0 * y0[e, T0:T1] + c1 * y1[e, T0:T1] + c2 * y2[e, T0:T1]
        r_out[s] = b[e, T0:T1] - (c0 * w1[s] + c1 * w2[e, T0:T1] + c2 * w3[s])

    for copies in tm_first + lon_first + cor_first + lon_late + lon_rows + [lon_y0, lon_y1, tm_y1, cor_y1, lon_u2, tm_u2]:
        copies.sent()
    for other, copy in gather:
        @pl.when(other)
        def _():
            copy.wait_send()

    @pl.when(collects)
    def _():
        for copy in exchange:
            copy.wait_send()

    @pl.when(spreads)
    def _():
        for copy in total_out:
            copy.wait_send()


def body(right_side, kappa_squared, hdiff, obs_weight):
    wide = pltpu.VMEM((EX, ET, NA), jnp.float32)
    block = pltpu.VMEM((NX, NT, NA), jnp.float32)
    dma = pltpu.SemaphoreType.DMA
    return pl.pallas_call(
        solve_kernel,
        out_shape=(jax.ShapeDtypeStruct((NX, NT, NA), jnp.float32),) * 2,
        in_specs=[pl.BlockSpec(memory_space=pl.ANY)] * 4,
        out_specs=(pl.BlockSpec(memory_space=pltpu.VMEM),) * 2,
        scratch_shapes=[wide] * 14 + [block] + [wide] + [block]
        + [pltpu.VMEM(shape, jnp.float32) for shape in (
            (2, NT, NA), (2, NT, NA), (2, 8, NA), (8, 128), (24, 1, 128), (32, 128), (1, 128))]
        + [dma((4,)), dma((6, 2)), dma((6, 2)), dma((11, 2)), dma((11, 2)), dma((5, 4)), dma((5, 4)),
           dma((2 * PLANES,)), dma((24,)), dma((32,)), dma((32,)), dma((REST,)), dma((1,))],
        compiler_params=pltpu.CompilerParams(
            collective_id=0, has_side_effects=True, vmem_limit_bytes=BUDGET
        ),
    )(right_side, kappa_squared, hdiff, obs_weight)


def solution(mesh):
    placed = P("lon", "tm", None)
    return jax.shard_map(
        body, mesh=mesh, in_specs=(placed,) * 4, out_specs=(placed,) * 2, check_vma=False
    )
```

```python
import itertools

import jax
import jax.numpy as jnp
from jax import lax
from jax.experimental import pallas as pl
from jax.experimental.pallas import tpu as pltpu
from jax.sharding import PartitionSpec as P

MESH = pl.DeviceIdType.MESH
SIZES = {"x": 4, "z": 12, "h": 2, "c": 2, "l": 4}
PLANES = 3
REST = 12 - PLANES
BUDGET = 107 * 2**19
NX, NT, NA = 8, 24, 256
HX, HT = 3, 8
EX, ET = NX + 2 * HX, NT + 2 * HT
T0, T1 = HT, HT + NT


def place():
    lon, tm = lax.axis_index("lon"), lax.axis_index("tm")
    return {"c": lon % 2, "h": (lon // 2) % 2, "z": (lon // 4) % 12, "x": lon // 48, "l": tm}


def peers(axes):
    here, out = place(), []
    lon, tm = lax.axis_index("lon"), lax.axis_index("tm")
    steps = {"x": 48, "z": 4, "h": 2, "c": 1}

    def moves(axis):
        at, size, step = here[axis], SIZES[axis], steps.get(axis, 1)
        return [0] + [step * (i - size * (at + i >= size).astype(jnp.int32)) for i in range(1, size)]

    shifts = {a: moves(a) for a in axes}
    for offset in itertools.product(*[range(SIZES[a]) for a in axes]):
        if any(offset):
            to_lon, to_tm = lon, tm
            for a, i in zip(axes, offset):
                if i and a == "l":
                    to_tm = to_tm + shifts[a][i]
                elif i:
                    to_lon = to_lon + shifts[a][i]
            out.append((to_lon, to_tm))
    return out


def face(here, there):
    total = here + there
    return jnp.where(total > 0, 2.0 * here * there / jnp.where(total > 0, total, 1.0), 0.0)


def roll(v, step, axis):
    return pltpu.roll(v, step % v.shape[axis], axis)


def solve_kernel(b_in, k_in, h_in, o_in, x_out, r_out,
                 b, k, h, o, fx, ft, fl, d, m, y0, y1, y2, u, v, w1, w2, w3, early, late, edge_k, edge_o, edge_g, outer, row, gathered, slots, total,
                 in_sem, s_tm, r_tm, s_lon, r_lon, s_cor, r_cor,
                 s_gather, r_gather, s_plane, r_plane, s_total, r_total):
    lon, tm = lax.axis_index("lon"), lax.axis_index("tm")
    east, west = lax.rem(lon + 1, 192), lax.rem(lon + 191, 192)
    up, down = lax.rem(tm + 1, 4), lax.rem(tm + 3, 4)

    barrier = pltpu.get_barrier_semaphore()
    near = [(east, tm), (west, tm), (lon, up), (lon, down), (east, up), (east, down), (west, up), (west, down)]
    for who in near:
        pl.semaphore_signal(barrier, inc=1, device_id=who, device_id_type=MESH)

    mine = [
        pltpu.make_async_copy(src, dst.at[pl.ds(HX, NX), pl.ds(T0, NT)], in_sem.at[i])
        for i, (src, dst) in enumerate(((b_in, b), (k_in, k), (h_in, h), (o_in, o)))
    ]
    for copy in mine:
        copy.start()

    here = place()
    z, core = here["z"], here["c"]
    collects = z < PLANES
    column0 = lon - z * 4 - core
    plane = peers(("x", "h", "l"))

    def column(at_z, at_core):
        return (column0 + at_z * 4 + at_core, tm)

    spreads = z == PLANES - 1
    spread = [PLANES + i for i in range(REST)]

    @pl.when(collects)
    def _():
        for who in plane + peers(("z", "c")):
            pl.semaphore_signal(barrier, inc=1, device_id=who, device_id_type=MESH)

    @pl.when(jnp.logical_not(collects))
    def _():
        pl.semaphore_signal(barrier, inc=1, device_id=column(PLANES - 1, core), device_id_type=MESH)

    edges = ((h, 0.0), (k, 1.0), (o, 1.0), (b, 0.0), (y1, 0.0), (v, 0.0))

    @pl.when(tm == 0)
    def _():
        for ref, value in edges:
            ref[:, :T0] = jnp.full((EX, HT, NA), value, jnp.float32)

    @pl.when(tm == 3)
    def _():
        for ref, value in edges:
            ref[:, T1:] = jnp.full((EX, HT, NA), value, jnp.float32)

    lat_own = lax.broadcasted_iota(jnp.int32, (NT, NA), 1)

    def own_y0(s):
        at = h[s, T0:T1]
        ftv = face(at, roll(at, -1, 0))
        flv = jnp.where(lat_own == NA - 1, 0.0, face(at, roll(at, -1, 1)))
        around = (face(at, h[s + 1, T0:T1]), face(h[s - 1, T0:T1], at), ftv, roll(ftv, 1, 0), flv, roll(flv, 1, 1))
        total, squares = k[s, T0:T1], o[s, T0:T1]
        for f in around:
            total += f
            squares += f * f
        return b[s, T0:T1] / (total * total + squares)

    for copy in mine:
        copy.wait()
    for side, (s, f) in enumerate(((HX + NX - 1, HX + NX - 2), (HX, HX))):
        inward = face(h[f, T0:T1], h[f + 1, T0:T1])
        edge_k[side] = k[s, T0:T1] + inward
        edge_o[side] = o[s, T0:T1] + inward * inward
        early[side] = inward * own_y0(HX + NX - 2 if side == 0 else HX + 1)

    @pl.when(collects)
    def _():
        pl.semaphore_wait(barrier, len(near) + 2 * PLANES - 1 + len(plane) + jnp.where(spreads, REST, 0))

    @pl.when(jnp.logical_not(collects))
    def _():
        pl.semaphore_wait(barrier, len(near) + 2 * PLANES)

    def remote(src, dst, ssem, rsem, who):
        return pltpu.make_async_remote_copy(src, dst, ssem, rsem, device_id=who, device_id_type=MESH)

    class Lon:
        def __init__(self, n, src, off_x, off_t, dst, depth, width=1):
            def part(at):
                return src.at[pl.ds(off_x + at, width), pl.ds(off_t, NT)]

            def halo(at):
                return dst.at[pl.ds(at, width), pl.ds(T0, NT)]

            self.copies = [
                remote(part(NX - depth - width + 1), halo(HX - depth - width + 1),
                       s_lon.at[n, 0], r_lon.at[n, 0], (east, tm)),
                remote(part(depth - 1), halo(HX + NX + depth - 1),
                       s_lon.at[n, 1], r_lon.at[n, 1], (west, tm)),
            ]

        def start(self):
            for copy in self.copies:
                copy.start()

        def received(self, side=None):
            for copy in self.copies if side is None else self.copies[side : side + 1]:
                copy.wait_recv()

        def sent(self):
            for copy in self.copies:
                copy.wait_send()

    class Tm:
        def __init__(self, upward, downward):
            self.upward, self.downward = upward, downward

        def run(self, what, towards, back, side=None):
            part = slice(None) if side is None else slice(side, side + 1)

            @pl.when(towards)
            def _():
                for copy in self.upward[part]:
                    getattr(copy, what)()

            @pl.when(back)
            def _():
                for copy in self.downward[part]:
                    getattr(copy, what)()

        def start(self):
            self.run("start", tm < 3, tm > 0)

        def received(self, side=None):
            self.run("wait_recv", tm > 0, tm < 3, side)

        def sent(self):
            self.run("wait_send", tm < 3, tm > 0)

    def rows(n, src, off_x, off_t, dst, width):
        return Tm(
            [remote(src.at[pl.ds(off_x, NX), pl.ds(off_t + NT - width, width)],
                    dst.at[pl.ds(HX, NX), pl.ds(T0 - width, width)], s_tm.at[n, 0], r_tm.at[n, 0], (lon, up))],
            [remote(src.at[pl.ds(off_x, NX), pl.ds(off_t, width)],
                    dst.at[pl.ds(HX, NX), pl.ds(T1, width)], s_tm.at[n, 1], r_tm.at[n, 1], (lon, down))],
        )

    def corners(n, src, off_x, off_t, dst, width):
        def make(i, sx, st, dx, dt, who):
            return remote(src.at[pl.ds(off_x + sx, width), pl.ds(off_t + st, width)],
                          dst.at[pl.ds(dx, width), pl.ds(dt, width)], s_cor.at[n, i], r_cor.at[n, i], who)

        return Tm(
            [make(0, NX - width, NT - width, HX - width, T0 - width, (east, up)),
             make(1, 0, NT - width, HX + NX, T0 - width, (west, up))],
            [make(2, NX - width, 0, HX - width, T1, (east, down)),
             make(3, 0, 0, HX + NX, T1, (west, down))],
        )

    def edge_corners(n, src, dst):
        def make(i, side, row_at, dx, dt, who):
            return remote(src.at[pl.ds(side, 1), pl.ds(row_at, 1)], dst.at[pl.ds(dx, 1), pl.ds(dt, 1)],
                          s_cor.at[n, i], r_cor.at[n, i], who)

        return Tm(
            [make(0, 0, NT - 1, HX - 1, T0 - 1, (east, up)), make(1, 1, NT - 1, HX + NX, T0 - 1, (west, up))],
            [make(2, 0, 0, HX - 1, T1, (east, down)), make(3, 1, 0, HX + NX, T1, (west, down))],
        )

    class Pair(Lon):
        def __init__(self, n, eastward, westward):
            self.copies = [
                remote(*eastward, s_lon.at[n, 0], r_lon.at[n, 0], (east, tm)),
                remote(*westward, s_lon.at[n, 1], r_lon.at[n, 1], (west, tm)),
            ]

    def edge_pair(n, src, dst):
        return Pair(n, (src.at[0], dst.at[HX - 1, pl.ds(T0, NT)]), (src.at[1], dst.at[HX + NX, pl.ds(T0, NT)]))

    inputs = ((h_in, h), (k_in, k), (o_in, o), (b_in, b))
    tm_first = [rows(i, src, 0, 0, dst, 3 if i == 0 else 2) for i, (src, dst) in enumerate(inputs)]
    lon_first = [
        Lon(0, h_in, 0, 0, h, 1), edge_pair(1, edge_k, k), edge_pair(2, edge_o, o), Lon(3, b_in, 0, 0, b, 1),
    ]
    cor_first = [
        corners(0, h_in, 0, 0, h, 2), edge_corners(1, edge_k, k), edge_corners(2, edge_o, o),
        corners(3, b_in, 0, 0, b, 1),
    ]
    lon_y0 = Pair(4, (early.at[0], late.at[0]), (early.at[1], late.at[1]))
    lon_rows = [
        Pair(9 + i, *((edge_g.at[side, pl.ds(at, 1)], outer.at[side, pl.ds(at, 1)]) for side in (0, 1)))
        for i, at in enumerate((0, 7))
    ]
    lon_late = [Lon(5, h_in, 0, 0, h, 2, 2), Lon(6, k_in, 0, 0, k, 2)]

    tm_first[0].start()
    lon_first[0].start()
    for i in (1, 2, 3):
        tm_first[i].start()
    for i in (1, 2, 3):
        lon_first[i].start()
    lon_y0.start()
    for copies in cor_first:
        copies.start()

    lat = lax.broadcasted_iota(jnp.int32, (ET, NA), 1)

    def stencil(field, s):
        here = field[s]
        ftv, flv = ft[s], fl[s]
        sides = fx[s] * field[s + 1] + fx[s - 1] * field[s - 1]
        sides += ftv * roll(here, -1, 0) + roll(ftv * here, 1, 0)
        sides += flv * roll(here, -1, 1) + roll(flv * here, 1, 1)
        return d[s] * here - sides

    def across(*slabs):
        for s in slabs:
            fx[s] = face(h[s], h[s + 1])

    def within(*slabs):
        for s in slabs:
            here = h[s]
            ft[s] = face(here, roll(here, -1, 0))
            fl[s] = jnp.where(lat == NA - 1, 0.0, face(here, roll(here, -1, 1)))

    def diagonal(*slabs, full=True):
        for s in slabs:
            ftv, flv = ft[s], fl[s]
            around = (fx[s], fx[s - 1], ftv, roll(ftv, 1, 0), flv, roll(flv, 1, 1))
            total = k[s]
            for f in around:
                total += f
            d[s] = total
            if full:
                squares = o[s]
                for f in around:
                    squares += f * f
                inverse = 1.0 / (total * total + squares)
                m[s] = inverse
                y0[s] = inverse * b[s]

    def apply(src, *slabs):
        for s in slabs:
            u[s] = stencil(src, s)

    def next_first(*slabs):
        for s in slabs:
            w = (stencil(u, s) + o[s] * y0[s])[T0:T1]
            w1[s - HX] = w
            y1[s, T0:T1] = m[s, T0:T1] * w

    def next_second(*slabs):
        for s in slabs:
            w = stencil(u, s) + o[s] * y1[s]
            w2[s] = w
            y2[s] = m[s] * w

    for copies in tm_first:
        copies.received()
    across(3, 4, 8, 9)
    within(4, 9)
    diagonal(4, 9)
    for side, (s, f) in enumerate(((9, 9), (4, 3))):
        edge_g[side, 0:1] = fx[f, T0 : T0 + 1] * y0[s, T0 : T0 + 1]
        edge_g[side, 7:8] = fx[f, T1 - 1 : T1] * y0[s, T1 - 1 : T1]
    for copies in lon_rows + lon_late:
        copies.start()
    across(5, 6, 7)
    within(3, 5, 6, 7, 8, 10)
    diagonal(5, 6, 7, 8)
    apply(y0, 5, 6, 7, 8)
    next_first(6, 7)

    lon_y1 = Lon(7, y1, HX, T0, y1, 1, 3)
    tm_y1 = rows(4, y1, HX, T0, y1, 3)
    cor_y1 = corners(4, y1, HX, T0, y1, 2)
    step = lax.broadcasted_iota(jnp.int32, (NT, NA), 0)

    def moments(sums, *slabs):
        for s in slabs:
            t = stencil(y2, s)[T0:T1]
            v[s, T0:T1] = t
            yy0, yy1, yy2 = y0[s, T0:T1], y1[s, T0:T1], y2[s, T0:T1]
            ww1, ww2 = w1[s - HX], w2[s, T0:T1]
            terms = (b[s, T0:T1] * yy0, yy0 * ww1, ww1 * yy1, ww1 * yy2, ww2 * yy2,
                     t * t + o[s, T0:T1] * yy2 * yy2)
            sums = [a + term for a, term in zip(sums, terms)]
        return sums

    def finish(order):
        for side in order:
            def at(i):
                return EX - 1 - i if side else i

            inward = EX - 2 - 2 if side else 2
            lon_first[0].received(side)
            cor_first[0].received(side)
            across(inward)
            within(at(2))
            diagonal(at(3))
            apply(y0, at(4))
            next_first(at(5))
            for i in (1, 2, 3):
                lon_first[i].received(side)
                cor_first[i].received(side)
            edge = at(2)
            ftv, flv = ft[edge], fl[edge]
            total, squares = k[edge], o[edge]
            for f in (fx[inward], ftv, roll(ftv, 1, 0), flv, roll(flv, 1, 1)):
                total += f
                squares += f * f
            d[edge] = total
            m[edge] = 1.0 / (total * total + squares)
            here = m[edge] * b[edge]
            y0[edge] = here
            apply(y0, at(3))
            next_first(at(4))
            for copies in [lon_y0] + lon_rows:
                copies.received(side)
            far = jnp.where(step == 0, outer[side, 0:1], late[side])
            far = jnp.where(step == NT - 1, outer[side, 7:8], far)
            sides = fx[inward] * y0[at(3)]
            sides += ftv * roll(here, -1, 0) + roll(ftv * here, 1, 0)
            sides += flv * roll(here, -1, 1) + roll(flv * here, 1, 1)
            u[edge, T0:T1] = (total * here - sides)[T0:T1] - far
            next_first(at(3))
            lon_y1.copies[1 - side].start()
        tm_y1.start()
        cor_y1.start()

        for copies in lon_late:
            copies.received()
        across(0, 1, 11, 12)
        for s, f in ((2, 1), (11, 11)):
            o[s, T0:T1] = o[s, T0:T1] - fx[f, T0:T1] * fx[f, T0:T1]
        within(1, 12)
        diagonal(1, 12, full=False)
        tm_y1.received()
        apply(y1, 4, 5, 6, 7, 8, 9)
        next_second(5, 6, 7, 8)
        sums = moments([jnp.zeros((NT, NA), jnp.float32)] * 6, 6, 7)
        for side in order:
            lon_y1.received(side)
            cor_y1.received(side)
            slabs = (12, 11, 10, 9, 8) if side else (1, 2, 3, 4, 5)
            apply(y1, *slabs[:3])
            next_second(*slabs[1:4])
            sums = moments(sums, *slabs[2:])
        lane = lax.broadcasted_iota(jnp.int32, (1, 128), 1)
        packed = jnp.zeros((1, 128), jnp.float32)
        for i, part in enumerate(sums):
            packed = jnp.where(lane == i, jnp.sum(part, keepdims=True), packed)
        row[pl.ds(0, 1)] = packed

    @pl.when(core == 1)
    def _():
        finish((0, 1))

    @pl.when(core == 0)
    def _():
        finish((1, 0))

    lon_u2 = Lon(8, v, HX, T0, v, 1)
    tm_u2 = rows(5, v, HX, T0, v, 1)
    targets = [(at_z, at_core) for at_z in range(PLANES) for at_core in range(2)]
    gather = []
    for i, (at_z, at_core) in enumerate(targets):
        back = z - at_z + 12 * (z < at_z).astype(jnp.int32)
        slot = back * 2 + jnp.where(core == at_core, 0, 1)
        gather.append((slot != 0, remote(
            row.at[pl.ds(0, 1)], gathered.at[slot], s_gather.at[i], r_gather.at[slot], column(at_z, at_core))))
    for other, copy in gather:
        @pl.when(other)
        def _():
            copy.start()

    lon_u2.start()
    tm_u2.start()

    exchange = [
        remote(row.at[pl.ds(1, 1)], slots.at[pl.ds(i, 1)], s_plane.at[i], r_plane.at[i], who)
        for i, who in enumerate(plane)
    ]
    total_out = [
        remote(total, total, s_total.at[i], r_total.at[0], column(at_z, core)) for i, at_z in enumerate(spread)
    ]

    @pl.when(collects)
    def _():
        value = row[pl.ds(0, 1)]
        for i in range(1, 24):
            remote(row.at[pl.ds(0, 1)], gathered.at[i], s_gather.at[0], r_gather.at[i], (east, tm)).wait_recv()
            value = value + gathered[i]
        row[pl.ds(1, 1)] = value
        for copy in exchange:
            copy.start()

    tm_u2.received()
    lon_u2.received()
    for s in range(HX, HX + NX):
        w3[s - HX] = (stencil(v, s) + o[s] * y2[s])[T0:T1]

    @pl.when(collects)
    def _():
        for copy in exchange:
            copy.wait_recv()
        total[...] = row[pl.ds(1, 1)] + jnp.sum(slots[: len(plane)], axis=0, keepdims=True)

        @pl.when(spreads)
        def _():
            for copy in total_out:
                copy.start()

    @pl.when(jnp.logical_not(collects))
    def _():
        total_out[0].wait_recv()

    packed = total[...]
    mu = [packed[:, i : i + 1] for i in range(6)]

    def form(c, shift):
        total = 0.0
        for i, a in enumerate(c):
            for j, e in enumerate(c):
                total = total + a * e * mu[i + j + shift]
        return total

    a0 = mu[0] / mu[1]
    rho1 = [jnp.ones_like(a0), -a0]
    rz1 = form(rho1, 0)
    beta0 = rz1 / mu[0]
    p1 = [1.0 + beta0, -a0]
    a1 = rz1 / form(p1, 1)
    rho2 = [jnp.ones_like(a0), -a0 - a1 * p1[0], -a1 * p1[1]]
    rz2 = form(rho2, 0)
    beta1 = rz2 / rz1
    p2 = [rho2[0] + beta1 * p1[0], rho2[1] + beta1 * p1[1], rho2[2]]
    a2 = rz2 / form(p2, 1)
    c = (a0 + a1 * p1[0] + a2 * p2[0], a1 * p1[1] + a2 * p2[1], a2 * p2[2])
    c0, c1, c2 = (jnp.broadcast_to(value, (NT, NA)) for value in c)
    for s in range(NX):
        e = s + HX
        x_out[s] = c0 * y0[e, T0:T1] + c1 * y1[e, T0:T1] + c2 * y2[e, T0:T1]
        r_out[s] = b[e, T0:T1] - (c0 * w1[s] + c1 * w2[e, T0:T1] + c2 * w3[s])

    for copies in tm_first + lon_first + cor_first + lon_late + lon_rows + [lon_y0, lon_y1, tm_y1, cor_y1, lon_u2, tm_u2]:
        copies.sent()
    for other, copy in gather:
        @pl.when(other)
        def _():
            copy.wait_send()

    @pl.when(collects)
    def _():
        for copy in exchange:
            copy.wait_send()

    @pl.when(spreads)
    def _():
        for copy in total_out:
            copy.wait_send()


def body(right_side, kappa_squared, hdiff, obs_weight):
    wide = pltpu.VMEM((EX, ET, NA), jnp.float32)
    block = pltpu.VMEM((NX, NT, NA), jnp.float32)
    dma = pltpu.SemaphoreType.DMA
    return pl.pallas_call(
        solve_kernel,
        out_shape=(jax.ShapeDtypeStruct((NX, NT, NA), jnp.float32),) * 2,
        in_specs=[pl.BlockSpec(memory_space=pl.ANY)] * 4,
        out_specs=(pl.BlockSpec(memory_space=pltpu.VMEM),) * 2,
        scratch_shapes=[wide] * 14 + [block] + [wide] + [block]
        + [pltpu.VMEM(shape, jnp.float32) for shape in (
            (2, NT, NA), (2, NT, NA), (2, NT, NA), (2, NT, NA), (2, 8, NA), (2, 8, NA), (8, 128), (24, 1, 128), (32, 128), (1, 128))]
        + [dma((4,)), dma((6, 2)), dma((6, 2)), dma((11, 2)), dma((11, 2)), dma((5, 4)), dma((5, 4)),
           dma((2 * PLANES,)), dma((24,)), dma((32,)), dma((32,)), dma((REST,)), dma((1,))],
        compiler_params=pltpu.CompilerParams(
            collective_id=0, has_side_effects=True, vmem_limit_bytes=BUDGET
        ),
    )(right_side, kappa_squared, hdiff, obs_weight)


def solution(mesh):
    placed = P("lon", "tm", None)
    return jax.shard_map(
        body, mesh=mesh, in_specs=(placed,) * 4, out_specs=(placed,) * 2, check_vma=False
    )
```
